32 devices in a mesh: dp: 16 (over z, y, core), tensor: 2 (over x).
Axes of the slice: x: 2, y: 2, z: 4, core: 2. Of those that a mesh axis runs over, the one named last changes fastest.
Arguments:
- x_in: bfloat16 [32768, 768], P(('dp', 'tensor')), may hold values from -6 to 6
- cotangent: bfloat16 [32768, 768], P(('dp', 'tensor')), may hold values from -6 to 6
- sequence_lengths: int32 [32], replicated, may hold values from 1 to 2047, as said below
- sequence_owner: int32 [32], replicated, may hold values from 0 to 15, as said below
- norm_gain: float32 [768], replicated, may hold values from 0.5 to 1.5
- proj_gate: bfloat16 [768, 1536], P('dp', 'tensor'), may hold values from -0.21875 to 0.21875
- proj_value: bfloat16 [768, 1536], P('dp', 'tensor'), may hold values from -0.21875 to 0.21875
- proj_bc: bfloat16 [768, 256], P('dp'), may hold values from -0.21875 to 0.21875
- proj_step: bfloat16 [768, 24], P('dp', 'tensor'), may hold values from -0.21875 to 0.21875
- proj_out: bfloat16 [1536, 768], P('tensor', 'dp'), may hold values from -0.15625 to 0.15625
- conv_value: float32 [4, 1536], P(None, 'tensor'), may hold values from -3 to 3
- conv_value_bias: float32 [1536], P('tensor'), may hold values from -1.5 to 1.5
- conv_bc: float32 [4, 256], replicated, may hold values from -3 to 3
- conv_bc_bias: float32 [256], replicated, may hold values from -1.5 to 1.5
- step_bias: float32 [24], P('tensor'), may hold values from -5 to -1
- decay_log: float32 [24], P('tensor'), may hold values from 0 to 2.77
- skip_gain: float32 [24], P('tensor'), may hold values from 0.1 to 1.9
- gate_gain: float32 [1536], P('tensor'), may hold values from 0.5 to 1.5
Outputs:
- block_out: bfloat16 [32768, 768], P(('dp', 'tensor'))
- grad_in: bfloat16 [32768, 768], P(('dp', 'tensor'))
- g_norm_gain: float32 [768], replicated
- g_proj_gate: float32 [768, 1536], P('dp', 'tensor')
- g_proj_value: float32 [768, 1536], P('dp', 'tensor')
- g_proj_bc: float32 [768, 256], P('dp')
- g_proj_step: float32 [768, 24], P('dp', 'tensor')
- g_proj_out: float32 [1536, 768], P('tensor', 'dp')
- g_conv_value: float32 [4, 1536], P(None, 'tensor')
- g_conv_value_bias: float32 [1536], P('tensor')
- g_conv_bc: float32 [4, 256], replicated
- g_conv_bc_bias: float32 [256], replicated
- g_step_bias: float32 [24], P('tensor')
- g_decay_log: float32 [24], P('tensor')
- g_skip_gain: float32 [24], P('tensor')
- g_gate_gain: float32 [1536], P('tensor')
The draws below stay inside these ranges and needn't reach their ends.
Inputs may be any that keep to these rules, and one draw needn't show every extreme that they name: `sequence_owner`: each index of dp owns exactly 2 sequences. `sequence_lengths`: the lengths of the sequences of one index of dp sum to at most 2048, and to exactly 2048 for some index.
All inputs are finite; a program needn't handle non-finite values.
Results may differ from the reference program's by a relative error of at most 0.0095.
Values may be sent and summed in bfloat16 or wider, within the bound.
A program may use at most 192 MiB of HBM per device.

```python
import jax
import jax.numpy as jnp
from jax import lax

D = 768
HEADS = 24
STATE = 128
KCONV = 4
BLOCK = 256
ROWS = 2048
SEQ_DEV = 2
INNER = 1536
TOKENS = 32768
N_DP = 16


def sequence_table(key):
    key_owner, key_fill, key_full, key_parts = jax.random.split(key, 4)
    owners = jax.random.permutation(key_owner, jnp.repeat(jnp.arange(N_DP, dtype=jnp.int32), SEQ_DEV, total_repeat_length=N_DP * SEQ_DEV))
    filled = jax.random.randint(key_fill, (N_DP,), ROWS // 4, ROWS + 1, dtype=jnp.int32)
    full_index = jax.random.randint(key_full, (), 0, N_DP, dtype=jnp.int32)
    is_full = jnp.arange(N_DP, dtype=jnp.int32) == full_index
    filled = jnp.where(is_full, ROWS, filled)
    parts = jax.random.randint(key_parts, (N_DP, SEQ_DEV), 1, 9, dtype=jnp.int32)
    running = jnp.cumsum(parts, axis=1, dtype=jnp.int32)
    totals = running[:, -1:]
    bounds = filled[:, None] * running // totals
    starts = jnp.concatenate([jnp.zeros((N_DP, 1), jnp.int32), bounds[:, :-1]], axis=1)
    lengths_dev = bounds - starts
    slot_index = jnp.arange(SEQ_DEV, dtype=jnp.int32)
    fixed_row = jnp.where(slot_index == SEQ_DEV - 1, ROWS - SEQ_DEV + 1, 1).astype(jnp.int32)
    lengths_dev = jnp.where(is_full[:, None], fixed_row[None, :], lengths_dev)
    indices = jnp.arange(N_DP * SEQ_DEV, dtype=jnp.int32)
    earlier = (owners[None, :] == owners[:, None]) & (indices[None, :] < indices[:, None])
    ranks = jnp.sum(earlier.astype(jnp.int32), axis=1, dtype=jnp.int32)
    return (lengths_dev[owners, ranks], owners)


def draw_sequence_lengths(key, part):
    table = sequence_table(key)
    return table[0]


def draw_sequence_owner(key, part):
    table = sequence_table(key)
    return table[1]


def levels(stream_key, shape, shards, low, high):
    def one(position, shards_of):
        draws = jax.random.uniform(jax.random.fold_in(jax.random.fold_in(stream_key, 6), position), (shards_of,), jnp.float32, low / len(shards), high / len(shards))
        return jnp.repeat(jnp.exp(draws), shape[position] // shards_of).reshape((-1,) + (1,) * (len(shape) - position - 1))

    gain = one(*shards[0])
    for cut in shards[1:]:
        gain = gain * one(*cut)
    return gain


def noise(rng, dims, width, bound, cuts=(), kind=jnp.bfloat16):
    level = levels(rng, dims, cuts, -0.22, 0.18) if cuts else 1.0
    values = jax.random.normal(rng, dims, jnp.float32) * width * level
    return jnp.minimum(jnp.maximum(values, -bound), bound).astype(kind)


def setup_inputs(seed: int = 0) -> dict:
    key_list = jax.random.split(jax.random.key(seed), 19)
    return {
        "x_in": noise(key_list[0], (TOKENS, D), 1.0, 6.0, ((0, 32),)),
        "cotangent": noise(key_list[1], (TOKENS, D), 1.0, 6.0, ((0, 32),)),
        "sequence_lengths": draw_sequence_lengths(jax.random.fold_in(key_list[18], 71), 0),
        "sequence_owner": draw_sequence_owner(jax.random.fold_in(key_list[18], 71), 0),
        "norm_gain": jnp.clip(1.0 + 0.1 * jax.random.normal(key_list[4], (D,), jnp.float32), 0.5, 1.5),
        "proj_gate": noise(key_list[5], (D, INNER), D ** -0.5, 0.21875, ((0, 16), (1, 2))),
        "proj_value": noise(key_list[6], (D, INNER), D ** -0.5, 0.21875, ((0, 16), (1, 2))),
        "proj_bc": noise(key_list[7], (D, 2 * STATE), D ** -0.5, 0.21875, ((0, 16),)),
        "proj_step": noise(key_list[8], (D, HEADS), D ** -0.5, 0.21875, ((0, 16), (1, 2))),
        "proj_out": noise(key_list[9], (INNER, D), INNER ** -0.5, 0.15625, ((0, 2), (1, 16))),
        "conv_value": noise(key_list[10], (KCONV, INNER), KCONV ** -0.5, 3.0, ((1, 2),), jnp.float32),
        "conv_value_bias": noise(key_list[11], (INNER,), 0.3, 1.5, ((0, 2),), jnp.float32),
        "conv_bc": noise(key_list[12], (KCONV, 2 * STATE), KCONV ** -0.5, 3.0, (), jnp.float32),
        "conv_bc_bias": noise(key_list[13], (2 * STATE,), 0.3, 1.5, (), jnp.float32),
        "step_bias": jnp.clip(-5.0 + 4.0 * jax.random.uniform(key_list[14], (HEADS,), jnp.float32) ** levels(key_list[14], (HEADS,), ((0, 2),), -0.2, 0.2), -5.0, -1.0),
        "decay_log": jnp.clip(2.77 * jax.random.uniform(key_list[15], (HEADS,), jnp.float32) ** levels(key_list[15], (HEADS,), ((0, 2),), -0.2, 0.2), 0.0, 2.77),
        "skip_gain": jnp.clip(1.0 + 0.18 * jax.random.normal(key_list[16], (HEADS,), jnp.float32), 0.1, 1.9),
        "gate_gain": jnp.clip(1.0 + 0.1 * jax.random.normal(key_list[17], (INNER,), jnp.float32), 0.5, 1.5),
    }


EPSILON = 1e-05
PRECISION = lax.Precision.HIGHEST

@jax.custom_vjp
def low(v):
    return lax.optimization_barrier(v.astype(jnp.bfloat16)).astype(jnp.float32)

@jax.custom_vjp
def low_back(v):
    return v

def low_keep(v):
    return (low(v), None)

def low_pass(kept, grad):
    return (grad,)

def back_keep(v):
    return (v, None)

def back_low(kept, grad):
    return (low(grad),)
low.defvjp(low_keep, low_pass)
low_back.defvjp(back_keep, back_low)

def matmul(left_side, right_side):
    return jnp.dot(left_side, right_side, precision=PRECISION, preferred_element_type=jnp.float32)

def segments(sequence_lengths, sequence_owner, device, row_count):
    owned = (sequence_owner == device).astype(jnp.int32)
    seq_ends = jnp.cumsum(sequence_lengths * owned, dtype=jnp.int32)
    positions = jnp.arange(row_count, dtype=jnp.int32)
    finished = (seq_ends[None, :] <= positions[:, None]) & (owned[None, :] == 1)
    segment = lax.optimization_barrier(jnp.sum(finished.astype(jnp.int32), axis=1, dtype=jnp.int32))
    present = positions < seq_ends[-1]
    return (segment, present)

def conv_seq(values, kernel, offset_bias, segment):
    kernel_size = kernel.shape[0]
    row_count = values.shape[0]
    result = offset_bias + kernel[kernel_size - 1] * values
    for offset in range(1, kernel_size):
        moved = jnp.pad(values[:row_count - offset], ((offset, 0), (0, 0)))
        before = jnp.pad(segment[:row_count - offset], (offset, 0), constant_values=-1)
        result = result + kernel[kernel_size - 1 - offset] * moved * (before == segment).astype(jnp.float32)[:, None]
    return result

def scan_heads(values, keys_b, query_c, step_size, decay_rate, segment):
    row_count, head_count, head_dim = values.shape
    state_size = keys_b.shape[1]
    blocks = row_count // BLOCK
    value_blocks = values.reshape(blocks, BLOCK, head_count, head_dim)
    step_blocks = step_size.reshape(blocks, BLOCK, head_count)
    key_blocks = keys_b.reshape(blocks, BLOCK, state_size)
    query_blocks = query_c.reshape(blocks, BLOCK, state_size)
    segment_blocks = segment.reshape(blocks, BLOCK)
    lower_mask = jnp.arange(BLOCK)[:, None] >= jnp.arange(BLOCK)[None, :]
    rates = step_blocks * decay_rate
    cum_rates = jnp.einsum('ij,cjh->cih', lower_mask.astype(jnp.float32), rates, precision=PRECISION)
    same_segment = lower_mask[None] & (segment_blocks[:, :, None] == segment_blocks[:, None, :])
    rate_gaps = cum_rates[:, :, None, :] - cum_rates[:, None, :, :]
    decays = jnp.exp(jnp.where(same_segment[..., None], rate_gaps, 0.0)) * same_segment.astype(jnp.float32)[..., None]
    scores = jnp.einsum('cin,cjn->cij', query_blocks, key_blocks, precision=PRECISION)
    score_weights = scores[..., None] * decays * step_blocks[:, None, :, :]
    inside = jnp.einsum('cijh,cjhp->cihp', score_weights, value_blocks, precision=PRECISION)
    last_rate = cum_rates[:, -1, :]
    tail_mask = (segment_blocks == segment_blocks[:, -1:]).astype(jnp.float32)
    tail_weight = jnp.exp(last_rate[:, None, :] - cum_rates) * tail_mask[..., None] * step_blocks
    states = jnp.einsum('cjh,cjhp,cjn->chpn', tail_weight, value_blocks, key_blocks, precision=PRECISION)
    prev_last = jnp.concatenate([jnp.full((1,), -2, jnp.int32), segment_blocks[:-1, -1]])
    keep_flag = (segment_blocks[:, -1] == prev_last).astype(jnp.float32)
    carry_gain = jnp.exp(last_rate) * keep_flag[:, None]

    def advance(carry_state, block_item):
        gain_now, fresh_state = block_item
        return (gain_now[:, None, None] * carry_state + fresh_state, carry_state)
    ended, prior_state = lax.scan(advance, jnp.zeros((head_count, head_dim, state_size), jnp.float32), (carry_gain, states))
    head_same = (segment_blocks == prev_last[:, None]).astype(jnp.float32)
    carried = jnp.einsum('cin,chpn->cihp', query_blocks, prior_state, precision=PRECISION)
    carried = carried * (jnp.exp(cum_rates) * head_same[..., None])[..., None]
    return (inside + carried).reshape(row_count, head_count, head_dim)

def mixer(value_proj, bc_proj, step_raw, conv_value, conv_value_bias, conv_bc, conv_bc_bias, step_bias, decay_log, skip_gain, segment):
    conv_out = jax.nn.silu(conv_seq(value_proj, conv_value, conv_value_bias, segment))
    bc_conv = jax.nn.silu(conv_seq(bc_proj, conv_bc, conv_bc_bias, segment))
    state_size = bc_proj.shape[1] // 2
    step_size = jax.nn.softplus(step_raw + step_bias)
    decay_rate = -jnp.exp(decay_log)
    row_count = value_proj.shape[0]
    head_count = step_size.shape[1]
    head_dim = value_proj.shape[1] // head_count
    values = conv_out.reshape(row_count, head_count, head_dim)
    mixed_out = scan_heads(values, bc_conv[:, :state_size], bc_conv[:, state_size:], step_size, decay_rate, segment)
    mixed_out = mixed_out + skip_gain[None, :, None] * values
    return mixed_out.reshape(row_count, head_count * head_dim)

def block_one(rows_in, params, segment, present):
    norm_gain, proj_gate, proj_value, proj_bc, proj_step, proj_out, conv_value, conv_value_bias, conv_bc, conv_bc_bias, step_bias, decay_log, skip_gain, gate_gain = params
    in_rstd = lax.rsqrt(lax.optimization_barrier(jnp.mean(rows_in * rows_in, axis=-1, keepdims=True)) + EPSILON)
    normed = low(rows_in * in_rstd * norm_gain)
    gate_z = low_back(matmul(normed, proj_gate))
    value_proj = low_back(matmul(normed, proj_value))
    bc_proj = low_back(matmul(normed, proj_bc))
    step_raw = low_back(matmul(normed, proj_step))
    mixed_out = mixer(value_proj, bc_proj, step_raw, conv_value, conv_value_bias, conv_bc, conv_bc_bias, step_bias, decay_log, skip_gain, segment)
    gated_out = mixed_out * jax.nn.silu(gate_z)
    gate_scale = lax.rsqrt(lax.optimization_barrier(jnp.mean(gated_out * gated_out, axis=-1, keepdims=True)) + EPSILON)
    gnorm = low(gated_out * gate_scale * gate_gain)
    branch = low_back(matmul(gnorm, proj_out))
    return rows_in + present[:, None] * branch

def reference(x_in, cotangent, sequence_lengths, sequence_owner, norm_gain, proj_gate, proj_value, proj_bc, proj_step, proj_out, conv_value, conv_value_bias, conv_bc, conv_bc_bias, step_bias, decay_log, skip_gain, gate_gain):
    params = tuple((item.astype(jnp.float32) for item in (norm_gain, proj_gate, proj_value, proj_bc, proj_step, proj_out, conv_value, conv_value_bias, conv_bc, conv_bc_bias, step_bias, decay_log, skip_gain, gate_gain)))
    inputs = x_in.astype(jnp.float32).reshape(N_DP, ROWS, D)
    cot_blocks = cotangent.astype(jnp.float32).reshape(N_DP, ROWS, D)

    def mark_rows(device):
        return segments(sequence_lengths, sequence_owner, device, ROWS)
    segment_all, present_all = lax.map(mark_rows, jnp.arange(N_DP, dtype=jnp.int32))
    present_float = present_all.astype(jnp.float32)
    saved_block = jax.checkpoint(block_one)

    def forward(weights_in, rows_all):

        def one_group(group_item):
            return saved_block(group_item[0], weights_in, group_item[1], group_item[2])
        return lax.map(one_group, (rows_all, segment_all, present_float))
    outputs, pullback = jax.vjp(forward, params, inputs)
    gradients, grad_inputs = pullback(cot_blocks)
    return (outputs.reshape(TOKENS, D).astype(jnp.bfloat16), grad_inputs.reshape(TOKENS, D).astype(jnp.bfloat16), gradients[0], gradients[1], gradients[2], gradients[3], gradients[4], gradients[5], gradients[6], gradients[7], gradients[8], gradients[9], gradients[10], gradients[11], gradients[12], gradients[13])
```

```python
from functools import partial

import jax
import jax.numpy as jnp
from jax import lax
from jax.sharding import PartitionSpec as P

BLOCK = 256


EPSILON = 1e-05
PRECISION = lax.Precision.DEFAULT
SUM_PRECISION = lax.Precision.HIGHEST


def segments(sequence_lengths, sequence_owner, device, row_count):
    owned = (sequence_owner == device).astype(jnp.int32)
    seq_ends = jnp.cumsum(sequence_lengths * owned, dtype=jnp.int32)
    positions = jnp.arange(row_count, dtype=jnp.int32)
    finished = (seq_ends[None, :] <= positions[:, None]) & (owned[None, :] == 1)
    segment = jnp.sum(finished.astype(jnp.int32), axis=1, dtype=jnp.int32)
    present = positions < seq_ends[-1]
    return (segment, present)


def conv_seq(values, kernel, offset_bias, segment):
    kernel_size = kernel.shape[0]
    row_count = values.shape[0]
    result = offset_bias + kernel[kernel_size - 1] * values
    for offset in range(1, kernel_size):
        moved = jnp.pad(values[: row_count - offset], ((offset, 0), (0, 0)))
        before = jnp.pad(segment[: row_count - offset], (offset, 0), constant_values=-1)
        result = (
            result
            + kernel[kernel_size - 1 - offset]
            * moved
            * (before == segment).astype(jnp.float32)[:, None]
        )
    return result


def scan_heads(values, keys_b, query_c, step_size, decay_rate, segment):
    row_count, head_count, head_dim = values.shape
    state_size = keys_b.shape[1]
    blocks = row_count // BLOCK
    value_blocks = values.reshape(blocks, BLOCK, head_count, head_dim)
    step_blocks = step_size.reshape(blocks, BLOCK, head_count)
    key_blocks = keys_b.reshape(blocks, BLOCK, state_size)
    query_blocks = query_c.reshape(blocks, BLOCK, state_size)
    segment_blocks = segment.reshape(blocks, BLOCK)
    lower_mask = jnp.arange(BLOCK)[:, None] >= jnp.arange(BLOCK)[None, :]
    rates = step_blocks * decay_rate
    cum_rates = jnp.einsum(
        "ij,cjh->cih", lower_mask.astype(jnp.float32), rates, precision=SUM_PRECISION
    )
    same_segment = lower_mask[None] & (segment_blocks[:, :, None] == segment_blocks[:, None, :])
    rate_gaps = cum_rates[:, :, None, :] - cum_rates[:, None, :, :]
    decays = (
        jnp.exp(jnp.where(same_segment[..., None], rate_gaps, 0.0))
        * same_segment.astype(jnp.float32)[..., None]
    )
    scores = jnp.einsum("cin,cjn->cij", query_blocks, key_blocks, precision=PRECISION)
    score_weights = scores[..., None] * decays * step_blocks[:, None, :, :]
    inside = jnp.einsum("cijh,cjhp->cihp", score_weights, value_blocks, precision=PRECISION)
    last_rate = cum_rates[:, -1, :]
    tail_mask = (segment_blocks == segment_blocks[:, -1:]).astype(jnp.float32)
    tail_weight = jnp.exp(last_rate[:, None, :] - cum_rates) * tail_mask[..., None] * step_blocks
    states = jnp.einsum(
        "cjh,cjhp,cjn->chpn", tail_weight, value_blocks, key_blocks, precision=PRECISION
    )
    prev_last = jnp.concatenate([jnp.full((1,), -2, jnp.int32), segment_blocks[:-1, -1]])
    keep_flag = (segment_blocks[:, -1] == prev_last).astype(jnp.float32)
    carry_gain = jnp.exp(last_rate) * keep_flag[:, None]

    def advance(carry_state, block_item):
        gain_now, fresh_state = block_item
        return (gain_now[:, None, None] * carry_state + fresh_state, carry_state)

    ended, prior_state = lax.scan(
        advance, jnp.zeros((head_count, head_dim, state_size), jnp.float32), (carry_gain, states)
    )
    head_same = (segment_blocks == prev_last[:, None]).astype(jnp.float32)
    carried = jnp.einsum("cin,chpn->cihp", query_blocks, prior_state, precision=PRECISION)
    carried = carried * (jnp.exp(cum_rates) * head_same[..., None])[..., None]
    return (inside + carried).reshape(row_count, head_count, head_dim)


def mixer(
    value_proj,
    bc_proj,
    step_raw,
    conv_value,
    conv_value_bias,
    conv_bc,
    conv_bc_bias,
    step_bias,
    decay_log,
    skip_gain,
    segment,
):
    conv_out = jax.nn.silu(conv_seq(value_proj, conv_value, conv_value_bias, segment))
    bc_conv = jax.nn.silu(conv_seq(bc_proj, conv_bc, conv_bc_bias, segment))
    state_size = bc_proj.shape[1] // 2
    step_size = jax.nn.softplus(step_raw + step_bias)
    decay_rate = -jnp.exp(decay_log)
    row_count = value_proj.shape[0]
    head_count = step_size.shape[1]
    head_dim = value_proj.shape[1] // head_count
    values = conv_out.reshape(row_count, head_count, head_dim)
    mixed_out = scan_heads(
        values, bc_conv[:, :state_size], bc_conv[:, state_size:], step_size, decay_rate, segment
    )
    mixed_out = mixed_out + skip_gain[None, :, None] * values
    return mixed_out.reshape(row_count, head_count * head_dim)


def contract_rows(left_side, right_side):
    return lax.dot_general(
        left_side, right_side, (((0,), (0,)), ((), ())), preferred_element_type=jnp.float32
    )


def contract_cols(left_side, right_side):
    return lax.dot_general(
        left_side, right_side, (((1,), (1,)), ((), ())), preferred_element_type=jnp.float32
    )


def widen(local_part, tensor_count, tensor_index):
    axis_last = local_part.ndim - 1
    width_local = local_part.shape[axis_last]
    shape_full = local_part.shape[:axis_last] + (width_local * tensor_count,)
    return lax.dynamic_update_slice_in_dim(
        jnp.zeros(shape_full, jnp.float32), local_part, tensor_index * width_local, axis_last
    )


def narrow(full_part, width_local, tensor_index):
    axis_last = full_part.ndim - 1
    return lax.dynamic_slice_in_dim(full_part, tensor_index * width_local, width_local, axis_last)


def body(
    x_in,
    cotangent,
    sequence_lengths,
    sequence_owner,
    norm_gain,
    proj_gate,
    proj_value,
    proj_bc,
    proj_step,
    proj_out,
    conv_value,
    conv_value_bias,
    conv_bc,
    conv_bc_bias,
    step_bias,
    decay_log,
    skip_gain,
    gate_gain,
):
    half_rows = x_in.shape[0]
    tensor_count = lax.axis_size("tensor")
    row_count = half_rows * tensor_count
    tensor_index = lax.axis_index("tensor")
    device_index = lax.axis_index("dp")
    inner_local = proj_gate.shape[1]
    heads_local = proj_step.shape[1]
    main_cols = 2 * inner_local + heads_local
    inner_all = inner_local * tensor_count
    in_float = x_in.astype(jnp.float32)
    in_rstd = lax.rsqrt(jnp.mean(in_float * in_float, axis=-1, keepdims=True) + EPSILON)
    in_hat = in_float * in_rstd
    normed = (in_hat * norm_gain).astype(jnp.bfloat16)
    side_pack = jnp.concatenate([proj_value, proj_step, proj_bc], 1)
    gate_pack = jnp.concatenate([proj_gate, proj_out.T], 1)
    side_weight = lax.all_gather(side_pack, "dp", axis=0, tiled=True)
    gate_pack = lax.all_gather(gate_pack, "dp", axis=0, tiled=True)
    gate_weight = gate_pack[:, :inner_local]
    out_weight = gate_pack[:, inner_local:]
    normed_all = lax.all_gather(normed, "tensor", axis=0, tiled=True)
    projected = jnp.dot(normed_all, side_weight, preferred_element_type=jnp.float32)
    value_proj = projected[:, :inner_local]
    step_raw = projected[:, inner_local : inner_local + heads_local]
    bc_proj = projected[:, inner_local + heads_local :]
    gate_z = jnp.dot(normed_all, gate_weight, preferred_element_type=jnp.float32)
    segment, present = segments(sequence_lengths, sequence_owner, device_index, row_count)
    present_float = present.astype(jnp.float32)
    mixed_out, mixer_back = jax.vjp(
        jax.checkpoint(partial(mixer, segment=segment)),
        value_proj,
        bc_proj,
        step_raw,
        conv_value,
        conv_value_bias,
        conv_bc,
        conv_bc_bias,
        step_bias,
        decay_log,
        skip_gain,
    )
    gate_sigmoid = jax.nn.sigmoid(gate_z)
    silu_gate = gate_z * gate_sigmoid
    gated_out = mixed_out * silu_gate
    squares = lax.psum(jnp.sum(gated_out * gated_out, axis=-1), "tensor")
    gate_scale = lax.rsqrt(squares / inner_all + EPSILON)[:, None]
    gnorm = (gated_out * gate_scale * gate_gain).astype(jnp.bfloat16)
    branch_own = lax.psum_scatter(
        contract_cols(gnorm, out_weight).astype(jnp.bfloat16),
        "tensor",
        scatter_dimension=0,
        tiled=True,
    ).astype(jnp.float32)
    present_own = lax.dynamic_slice_in_dim(present_float, tensor_index * half_rows, half_rows, 0)
    block_out = (in_float + present_own[:, None] * branch_own).astype(jnp.bfloat16)
    mask_rows = present_float.astype(jnp.bfloat16)
    masked_cot = lax.all_gather(cotangent, "tensor", axis=0, tiled=True) * mask_rows[:, None]
    part_rows = jnp.dot(masked_cot, out_weight, preferred_element_type=jnp.float32)
    gated_scaled = gated_out * gate_scale
    grad_gate_gain = jnp.sum(part_rows * gated_scaled, axis=0)
    grad_hat = part_rows * gate_gain
    dot_sums = lax.psum(jnp.sum(grad_hat * gated_out, axis=-1), "tensor")
    grad_gated = (
        gate_scale * grad_hat
        - gated_out * (gate_scale * gate_scale * gate_scale) * (dot_sums / inner_all)[:, None]
    )
    grad_mixed = grad_gated * silu_gate
    grad_gate_z = grad_gated * mixed_out * gate_sigmoid * (1.0 + gate_z * (1.0 - gate_sigmoid))
    (
        grad_value,
        grad_bc_part,
        grad_step,
        g_conv_value,
        g_conv_value_bias,
        g_conv_bc,
        g_conv_bc_bias,
        g_step_bias,
        g_decay_log,
        g_skip_gain,
    ) = mixer_back(grad_mixed)
    grad_gate_z = grad_gate_z.astype(jnp.bfloat16)
    early = jnp.concatenate(
        [contract_rows(normed_all, grad_gate_z), contract_rows(masked_cot, gnorm)], 1
    ).astype(jnp.bfloat16)
    early = lax.psum_scatter(early, "dp", scatter_dimension=0, tiled=True).astype(jnp.float32)
    bc_own = lax.psum_scatter(
        grad_bc_part.astype(jnp.bfloat16), "tensor", scatter_dimension=0, tiled=True
    )
    grad_main = jnp.concatenate([grad_value, grad_step], 1).astype(jnp.bfloat16)
    late = jnp.concatenate(
        [contract_rows(normed_all, grad_main), contract_rows(normed, bc_own)], 1
    ).astype(jnp.bfloat16)
    late = lax.psum_scatter(late, "dp", scatter_dimension=0, tiled=True).astype(jnp.float32)
    side_cols = inner_local + heads_local
    grad_normed = lax.psum_scatter(
        (
            contract_cols(grad_gate_z, gate_weight)
            + contract_cols(grad_main, side_weight[:, :side_cols])
        ).astype(jnp.bfloat16),
        "tensor",
        scatter_dimension=0,
        tiled=True,
    ).astype(jnp.float32) + contract_cols(bc_own, side_weight[:, side_cols:])
    summed = (
        early[:, :inner_local],
        late[:, :inner_local],
        lax.psum(late[:, side_cols:], "tensor"),
        late[:, inner_local:side_cols],
        early[:, inner_local:].T,
    )
    grad_hat_in = grad_normed * norm_gain
    grad_in = in_rstd * (
        grad_hat_in - in_hat * jnp.mean(grad_hat_in * in_hat, axis=-1, keepdims=True)
    )
    grad_in = (grad_in + cotangent.astype(jnp.float32)).astype(jnp.bfloat16)
    gain_part = jnp.sum(grad_normed * in_hat, axis=0)
    small = lax.psum(
        (
            gain_part,
            g_conv_bc,
            g_conv_bc_bias,
            widen(g_conv_value, tensor_count, tensor_index),
            widen(g_conv_value_bias, tensor_count, tensor_index),
            widen(g_step_bias, tensor_count, tensor_index),
            widen(g_decay_log, tensor_count, tensor_index),
            widen(g_skip_gain, tensor_count, tensor_index),
            widen(grad_gate_gain, tensor_count, tensor_index),
        ),
        ("dp", "tensor"),
    )
    return (
        block_out,
        grad_in,
        small[0],
        summed[0],
        summed[1],
        summed[2],
        summed[3],
        summed[4],
        narrow(small[3], inner_local, tensor_index),
        narrow(small[4], inner_local, tensor_index),
        small[1],
        small[2],
        narrow(small[5], heads_local, tensor_index),
        narrow(small[6], heads_local, tensor_index),
        narrow(small[7], heads_local, tensor_index),
        narrow(small[8], inner_local, tensor_index),
    )


def solution(mesh):
    in_specs = (
        P(("dp", "tensor"), None),
        P(("dp", "tensor"), None),
        P(),
        P(),
        P(),
        P("dp", "tensor"),
        P("dp", "tensor"),
        P("dp", None),
        P("dp", "tensor"),
        P("tensor", "dp"),
        P(None, "tensor"),
        P("tensor"),
        P(),
        P(),
        P("tensor"),
        P("tensor"),
        P("tensor"),
        P("tensor"),
    )
    out_specs = (
        P(("dp", "tensor"), None),
        P(("dp", "tensor"), None),
        P(),
        P("dp", "tensor"),
        P("dp", "tensor"),
        P("dp", None),
        P("dp", "tensor"),
        P("tensor", "dp"),
        P(None, "tensor"),
        P("tensor"),
        P(),
        P(),
        P("tensor"),
        P("tensor"),
        P("tensor"),
        P("tensor"),
    )
    return jax.shard_map(body, mesh=mesh, in_specs=in_specs, out_specs=out_specs, check_vma=False)
```

```python
from functools import partial

import jax
import jax.numpy as jnp
from jax import lax
from jax.experimental import pallas as pl
from jax.experimental.pallas import tpu as pltpu
from jax.sharding import PartitionSpec as P

BLOCK = 256


EPSILON = 1e-05
SUM_PRECISION = lax.Precision.HIGHEST


def segments(sequence_lengths, sequence_owner, device, row_count):
    owned = (sequence_owner == device).astype(jnp.int32)
    seq_ends = jnp.cumsum(sequence_lengths * owned, dtype=jnp.int32)
    positions = jnp.arange(row_count, dtype=jnp.int32)
    finished = (seq_ends[None, :] <= positions[:, None]) & (owned[None, :] == 1)
    segment = jnp.sum(finished.astype(jnp.int32), axis=1, dtype=jnp.int32)
    present = positions < seq_ends[-1]
    return (segment, present)


def conv_seq(values, kernel, offset_bias, segment):
    kernel_size = kernel.shape[0]
    row_count = values.shape[0]
    result = offset_bias + kernel[kernel_size - 1] * values
    for offset in range(1, kernel_size):
        moved = jnp.pad(values[: row_count - offset], ((offset, 0), (0, 0)))
        before = jnp.pad(segment[: row_count - offset], (offset, 0), constant_values=-1)
        result = (
            result
            + kernel[kernel_size - 1 - offset]
            * moved
            * (before == segment).astype(jnp.float32)[:, None]
        )
    return result


def prepare(
    value_proj,
    bc_proj,
    step_raw,
    conv_value,
    conv_value_bias,
    conv_bc,
    conv_bc_bias,
    step_bias,
    decay_log,
    segment,
):
    values = jax.nn.silu(conv_seq(value_proj, conv_value, conv_value_bias, segment))
    bc_conv = jax.nn.silu(conv_seq(bc_proj, conv_bc, conv_bc_bias, segment))
    state_size = bc_proj.shape[1] // 2
    step_size = jax.nn.softplus(step_raw + step_bias)
    row_count, head_count = step_size.shape
    blocks = row_count // BLOCK
    rates = (step_size * -jnp.exp(decay_log)).reshape(blocks, BLOCK, head_count)
    segment_blocks = segment.reshape(blocks, BLOCK)
    lower_mask = jnp.arange(BLOCK)[:, None] >= jnp.arange(BLOCK)[None, :]
    cum_rates = jnp.einsum(
        "ij,cjh->cih", lower_mask.astype(jnp.float32), rates, precision=SUM_PRECISION
    )
    last_rate = cum_rates[:, -1, :]
    prev_last = jnp.concatenate([jnp.full((1,), -2, jnp.int32), segment_blocks[:-1, -1]])
    tail_mask = (segment_blocks == segment_blocks[:, -1:]).astype(jnp.float32)
    head_same = (segment_blocks == prev_last[:, None]).astype(jnp.float32)
    keep_flag = (segment_blocks[:, -1] == prev_last).astype(jnp.float32)
    tail = jnp.exp(last_rate[:, None, :] - cum_rates) * tail_mask[..., None]
    edge = jnp.exp(cum_rates) * head_same[..., None]
    gain = jnp.exp(last_rate) * keep_flag[:, None]
    flat = (row_count, head_count)
    return (
        values,
        bc_conv[:, :state_size],
        bc_conv[:, state_size:],
        step_size,
        cum_rates.reshape(flat),
        edge.reshape(flat),
        tail.reshape(flat),
        jnp.repeat(gain, values.shape[1] // head_count, axis=1)[:, None, :],
    )


def block_mask(seg_col, seg_row):
    shape = (BLOCK, BLOCK)
    lower = lax.broadcasted_iota(jnp.int32, shape, 0) >= lax.broadcasted_iota(jnp.int32, shape, 1)
    return lower & (seg_col[...] == seg_row[...])


def pick(ref, pair, low_lane):
    return jnp.where(low_lane, ref[:, 2 * pair : 2 * pair + 1], ref[:, 2 * pair + 1 : 2 * pair + 2])


def scan_forward_kernel(
    v, b, c, step, cum, edge, tail, gain, cum_row, seg_col, seg_row, skip, y, prior, state
):
    @pl.when(pl.program_id(0) == 0)
    def _():
        state[...] = jnp.zeros_like(state)

    prior[...] = state[...]
    keys = b[...].astype(jnp.bfloat16)
    queries = c[...].astype(jnp.bfloat16)
    scores = contract_cols(queries, keys)
    mask = block_mask(seg_col, seg_row)
    low_lane = lax.broadcasted_iota(jnp.int32, (BLOCK, 128), 1) < 64
    for pair in range(v.shape[1] // 128):
        cols = slice(128 * pair, 128 * pair + 128)
        values = v[:, cols]
        scaled = values * pick(step, pair, low_lane)
        scaled_low = scaled.astype(jnp.bfloat16)
        inside = []
        for head in (2 * pair, 2 * pair + 1):
            gap = cum[:, head : head + 1] - cum_row[head : head + 1, :]
            weight = scores * jnp.exp(jnp.where(mask, gap, -1e30))
            inside.append(dot_rows(weight.astype(jnp.bfloat16), scaled_low))
        before = state[:, cols]
        carried = dot_rows(queries, before.astype(jnp.bfloat16)) * pick(edge, pair, low_lane)
        y[:, cols] = jnp.where(low_lane, inside[0], inside[1]) + carried + skip[:, cols] * values
        fresh = (scaled * pick(tail, pair, low_lane)).astype(jnp.bfloat16)
        state[:, cols] = gain[0, :, cols] * before + contract_rows(keys, fresh)


def scan_backward_kernel(
    v,
    b,
    c,
    step,
    cum,
    edge,
    tail,
    gain,
    cum_row,
    seg_col,
    seg_row,
    skip,
    dy,
    prior,
    dv,
    db,
    dc,
    dstep,
    dcum,
    dedge,
    dtail,
    dgain,
    dcum_row,
    dskip,
    dstate,
):
    @pl.when(pl.program_id(0) == 0)
    def _():
        dstate[...] = jnp.zeros_like(dstate)

    keys = b[...].astype(jnp.bfloat16)
    queries = c[...].astype(jnp.bfloat16)
    scores = contract_cols(queries, keys)
    mask = block_mask(seg_col, seg_row)
    low_lane = lax.broadcasted_iota(jnp.int32, (BLOCK, 128), 1) < 64
    dscores = jnp.zeros((BLOCK, BLOCK), jnp.float32)
    dqueries = jnp.zeros(c.shape, jnp.float32)
    dkeys = jnp.zeros(b.shape, jnp.float32)

    def put(ref, pair, product):
        low_part = jnp.sum(jnp.where(low_lane, product, 0.0), axis=1, keepdims=True)
        all_part = jnp.sum(product, axis=1, keepdims=True)
        ref[:, 2 * pair : 2 * pair + 1] = low_part
        ref[:, 2 * pair + 1 : 2 * pair + 2] = all_part - low_part

    for pair in range(v.shape[1] // 128):
        cols = slice(128 * pair, 128 * pair + 128)
        values = v[:, cols]
        grad = dy[:, cols]
        step_pair = pick(step, pair, low_lane)
        edge_pair = pick(edge, pair, low_lane)
        tail_pair = pick(tail, pair, low_lane)
        scaled = values * step_pair
        scaled_low = scaled.astype(jnp.bfloat16)
        grad_low = grad.astype(jnp.bfloat16)
        inside = []
        for side in range(2):
            head = 2 * pair + side
            gap = cum[:, head : head + 1] - cum_row[head : head + 1, :]
            decay = jnp.exp(jnp.where(mask, gap, -1e30))
            weight = scores * decay
            own = low_lane if side == 0 else jnp.logical_not(low_lane)
            dweight = contract_cols(jnp.where(own, grad, 0.0).astype(jnp.bfloat16), scaled_low)
            dscores = dscores + dweight * decay
            product = dweight * weight
            dcum[:, head : head + 1] = jnp.sum(product, axis=1, keepdims=True)
            dcum_row[head : head + 1, :] = jnp.sum(product, axis=0, keepdims=True)
            inside.append(contract_rows(weight.astype(jnp.bfloat16), grad_low))
        before = prior[:, cols]
        before_low = before.astype(jnp.bfloat16)
        after = dstate[:, cols]
        after_low = after.astype(jnp.bfloat16)
        put(dedge, pair, grad * dot_rows(queries, before_low))
        key_part = dot_rows(keys, after_low)
        put(dtail, pair, scaled * key_part)
        dscaled = jnp.where(low_lane, inside[0], inside[1]) + tail_pair * key_part
        put(dstep, pair, dscaled * values)
        dv[:, cols] = step_pair * dscaled + skip[:, cols] * grad
        dgain[0, :, cols] = jnp.sum(before * after, axis=0, keepdims=True)
        dskip[0, :, cols] = jnp.sum(grad * values, axis=0, keepdims=True)
        edge_grad = (edge_pair * grad).astype(jnp.bfloat16)
        dqueries = dqueries + contract_cols(edge_grad, before_low)
        dkeys = dkeys + contract_cols((tail_pair * scaled).astype(jnp.bfloat16), after_low)
        dstate[:, cols] = gain[0, :, cols] * after + contract_rows(queries, edge_grad)
    dscores_low = dscores.astype(jnp.bfloat16)
    dc[...] = dqueries + dot_rows(dscores_low, keys)
    db[...] = dkeys + contract_rows(dscores_low, queries)


def scan_specs(rows, width, heads, states, turned):
    blocks = rows // BLOCK

    def at(position):
        return blocks - 1 - position if turned else position

    wide = pl.BlockSpec((BLOCK, width), lambda i: (at(i), 0))
    key = pl.BlockSpec((BLOCK, states), lambda i: (at(i), 0))
    head = pl.BlockSpec((BLOCK, heads), lambda i: (at(i), 0))
    line = pl.BlockSpec((1, 1, width), lambda i: (at(i), 0, 0))
    across = pl.BlockSpec((heads, BLOCK), lambda i: (0, at(i)))
    seg_col = pl.BlockSpec((BLOCK, 1), lambda i: (at(i), 0))
    seg_row = pl.BlockSpec((1, BLOCK), lambda i: (0, at(i)))
    fixed = pl.BlockSpec((1, width), lambda i: (0, 0))
    prior = pl.BlockSpec((states, width), lambda i: (at(i), 0))
    inputs = [wide, key, key, head, head, head, head, line, across, seg_col, seg_row, fixed]
    return inputs, wide, key, head, line, across, prior


def f32(*shape):
    return jax.ShapeDtypeStruct(shape, jnp.float32)


def scan_forward(parts, extra):
    rows, width = parts[0].shape
    states, heads = parts[1].shape[1], parts[3].shape[1]
    blocks = rows // BLOCK
    inputs, wide, key, head, line, across, prior = scan_specs(rows, width, heads, states, False)
    return pl.pallas_call(
        scan_forward_kernel,
        grid=(blocks,),
        in_specs=inputs,
        out_specs=[wide, prior],
        out_shape=[f32(rows, width), f32(blocks * states, width)],
        scratch_shapes=[pltpu.VMEM((states, width), jnp.float32)],
        compiler_params=pltpu.CompilerParams(vmem_limit_bytes=48 * 1024 * 1024),
        name="scan_forward",
    )(*parts, *extra)


def scan_backward(parts, extra, grad_mixed, prior_states):
    rows, width = parts[0].shape
    states, heads = parts[1].shape[1], parts[3].shape[1]
    blocks = rows // BLOCK
    inputs, wide, key, head, line, across, prior = scan_specs(rows, width, heads, states, True)
    return pl.pallas_call(
        scan_backward_kernel,
        grid=(blocks,),
        in_specs=inputs + [wide, prior],
        out_specs=[wide, key, key, head, head, head, head, line, across, line],
        out_shape=[
            f32(rows, width),
            f32(rows, states),
            f32(rows, states),
            f32(rows, heads),
            f32(rows, heads),
            f32(rows, heads),
            f32(rows, heads),
            f32(blocks, 1, width),
            f32(heads, rows),
            f32(blocks, 1, width),
        ],
        scratch_shapes=[pltpu.VMEM((states, width), jnp.float32)],
        compiler_params=pltpu.CompilerParams(vmem_limit_bytes=48 * 1024 * 1024),
        name="scan_backward",
    )(*parts, *extra, grad_mixed, prior_states)


def dot_rows(left_side, right_side):
    return jnp.dot(left_side, right_side, preferred_element_type=jnp.float32)


def contract_rows(left_side, right_side):
    return lax.dot_general(
        left_side, right_side, (((0,), (0,)), ((), ())), preferred_element_type=jnp.float32
    )


def contract_cols(left_side, right_side):
    return lax.dot_general(
        left_side, right_side, (((1,), (1,)), ((), ())), preferred_element_type=jnp.float32
    )


def widen(local_part, tensor_count, tensor_index):
    axis_last = local_part.ndim - 1
    width_local = local_part.shape[axis_last]
    shape_full = local_part.shape[:axis_last] + (width_local * tensor_count,)
    return lax.dynamic_update_slice_in_dim(
        jnp.zeros(shape_full, jnp.float32), local_part, tensor_index * width_local, axis_last
    )


def narrow(full_part, width_local, tensor_index):
    axis_last = full_part.ndim - 1
    return lax.dynamic_slice_in_dim(full_part, tensor_index * width_local, width_local, axis_last)


def body(
    x_in,
    cotangent,
    sequence_lengths,
    sequence_owner,
    norm_gain,
    proj_gate,
    proj_value,
    proj_bc,
    proj_step,
    proj_out,
    conv_value,
    conv_value_bias,
    conv_bc,
    conv_bc_bias,
    step_bias,
    decay_log,
    skip_gain,
    gate_gain,
):
    half_rows = x_in.shape[0]
    tensor_count = lax.axis_size("tensor")
    row_count = half_rows * tensor_count
    tensor_index = lax.axis_index("tensor")
    device_index = lax.axis_index("dp")
    inner_local = proj_gate.shape[1]
    heads_local = proj_step.shape[1]
    main_cols = 2 * inner_local + heads_local
    inner_all = inner_local * tensor_count
    in_float = x_in.astype(jnp.float32)
    in_rstd = lax.rsqrt(jnp.mean(in_float * in_float, axis=-1, keepdims=True) + EPSILON)
    in_hat = in_float * in_rstd
    normed = (in_hat * norm_gain).astype(jnp.bfloat16)
    side_pack = jnp.concatenate([proj_value, proj_step, proj_bc], 1)
    gate_pack = jnp.concatenate([proj_gate, proj_out.T], 1)
    side_weight = lax.all_gather(side_pack, "dp", axis=0, tiled=True)
    gate_pack = lax.all_gather(gate_pack, "dp", axis=0, tiled=True)
    gate_weight = gate_pack[:, :inner_local]
    out_weight = gate_pack[:, inner_local:]
    normed_all = lax.all_gather(normed, "tensor", axis=0, tiled=True)
    projected = jnp.dot(normed_all, side_weight, preferred_element_type=jnp.float32)
    value_proj = projected[:, :inner_local]
    step_raw = projected[:, inner_local : inner_local + heads_local]
    bc_proj = projected[:, inner_local + heads_local :]
    gate_z = jnp.dot(normed_all, gate_weight, preferred_element_type=jnp.float32)
    segment, present = segments(sequence_lengths, sequence_owner, device_index, row_count)
    present_float = present.astype(jnp.float32)
    parts, prepare_back = jax.vjp(
        partial(prepare, segment=segment),
        value_proj,
        bc_proj,
        step_raw,
        conv_value,
        conv_value_bias,
        conv_bc,
        conv_bc_bias,
        step_bias,
        decay_log,
    )
    extra = (
        parts[4].T,
        segment[:, None],
        segment[None, :],
        jnp.repeat(skip_gain, inner_local // heads_local)[None, :],
    )
    mixed_out, prior_states = scan_forward(parts, extra)
    gate_sigmoid = jax.nn.sigmoid(gate_z)
    silu_gate = gate_z * gate_sigmoid
    gated_out = mixed_out * silu_gate
    squares = lax.psum(jnp.sum(gated_out * gated_out, axis=-1), "tensor")
    gate_scale = lax.rsqrt(squares / inner_all + EPSILON)[:, None]
    gnorm = (gated_out * gate_scale * gate_gain).astype(jnp.bfloat16)
    branch_own = lax.psum_scatter(
        contract_cols(gnorm, out_weight).astype(jnp.bfloat16),
        "tensor",
        scatter_dimension=0,
        tiled=True,
    ).astype(jnp.float32)
    present_own = lax.dynamic_slice_in_dim(present_float, tensor_index * half_rows, half_rows, 0)
    block_out = (in_float + present_own[:, None] * branch_own).astype(jnp.bfloat16)
    mask_rows = present_float.astype(jnp.bfloat16)
    masked_cot = lax.all_gather(cotangent, "tensor", axis=0, tiled=True) * mask_rows[:, None]
    part_rows = jnp.dot(masked_cot, out_weight, preferred_element_type=jnp.float32)
    gated_scaled = gated_out * gate_scale
    grad_gate_gain = jnp.sum(part_rows * gated_scaled, axis=0)
    grad_hat = part_rows * gate_gain
    dot_sums = lax.psum(jnp.sum(grad_hat * gated_out, axis=-1), "tensor")
    grad_gated = (
        gate_scale * grad_hat
        - gated_out * (gate_scale * gate_scale * gate_scale) * (dot_sums / inner_all)[:, None]
    )
    grad_mixed = grad_gated * silu_gate
    grad_gate_z = grad_gated * mixed_out * gate_sigmoid * (1.0 + gate_z * (1.0 - gate_sigmoid))
    *part_grads, dcum_row, dskip = scan_backward(parts, extra, grad_mixed, prior_states)
    part_grads[4] = part_grads[4] - dcum_row.T
    (
        grad_value,
        grad_bc_part,
        grad_step,
        g_conv_value,
        g_conv_value_bias,
        g_conv_bc,
        g_conv_bc_bias,
        g_step_bias,
        g_decay_log,
    ) = prepare_back(tuple(part_grads))
    g_skip_gain = jnp.sum(dskip.reshape(-1, heads_local, inner_local // heads_local), axis=(0, 2))
    grad_gate_z = grad_gate_z.astype(jnp.bfloat16)
    early = jnp.concatenate(
        [contract_rows(normed_all, grad_gate_z), contract_rows(masked_cot, gnorm)], 1
    ).astype(jnp.bfloat16)
    early = lax.psum_scatter(early, "dp", scatter_dimension=0, tiled=True).astype(jnp.float32)
    bc_own = lax.psum_scatter(
        grad_bc_part.astype(jnp.bfloat16), "tensor", scatter_dimension=0, tiled=True
    )
    grad_main = jnp.concatenate([grad_value, grad_step], 1).astype(jnp.bfloat16)
    late = jnp.concatenate(
        [contract_rows(normed_all, grad_main), contract_rows(normed, bc_own)], 1
    ).astype(jnp.bfloat16)
    late = lax.psum_scatter(late, "dp", scatter_dimension=0, tiled=True).astype(jnp.float32)
    side_cols = inner_local + heads_local
    grad_normed = lax.psum_scatter(
        (
            contract_cols(grad_gate_z, gate_weight)
            + contract_cols(grad_main, side_weight[:, :side_cols])
        ).astype(jnp.bfloat16),
        "tensor",
        scatter_dimension=0,
        tiled=True,
    ).astype(jnp.float32) + contract_cols(bc_own, side_weight[:, side_cols:])
    summed = (
        early[:, :inner_local],
        late[:, :inner_local],
        lax.psum(late[:, side_cols:], "tensor"),
        late[:, inner_local:side_cols],
        early[:, inner_local:].T,
    )
    grad_hat_in = grad_normed * norm_gain
    grad_in = in_rstd * (
        grad_hat_in - in_hat * jnp.mean(grad_hat_in * in_hat, axis=-1, keepdims=True)
    )
    grad_in = (grad_in + cotangent.astype(jnp.float32)).astype(jnp.bfloat16)
    gain_part = jnp.sum(grad_normed * in_hat, axis=0)
    small = lax.psum(
        (
            gain_part,
            g_conv_bc,
            g_conv_bc_bias,
            widen(g_conv_value, tensor_count, tensor_index),
            widen(g_conv_value_bias, tensor_count, tensor_index),
            widen(g_step_bias, tensor_count, tensor_index),
            widen(g_decay_log, tensor_count, tensor_index),
            widen(g_skip_gain, tensor_count, tensor_index),
            widen(grad_gate_gain, tensor_count, tensor_index),
        ),
        ("dp", "tensor"),
    )
    return (
        block_out,
        grad_in,
        small[0],
        summed[0],
        summed[1],
        summed[2],
        summed[3],
        summed[4],
        narrow(small[3], inner_local, tensor_index),
        narrow(small[4], inner_local, tensor_index),
        small[1],
        small[2],
        narrow(small[5], heads_local, tensor_index),
        narrow(small[6], heads_local, tensor_index),
        narrow(small[7], heads_local, tensor_index),
        narrow(small[8], inner_local, tensor_index),
    )


def solution(mesh):
    in_specs = (
        P(("dp", "tensor"), None),
        P(("dp", "tensor"), None),
        P(),
        P(),
        P(),
        P("dp", "tensor"),
        P("dp", "tensor"),
        P("dp", None),
        P("dp", "tensor"),
        P("tensor", "dp"),
        P(None, "tensor"),
        P("tensor"),
        P(),
        P(),
        P("tensor"),
        P("tensor"),
        P("tensor"),
        P("tensor"),
    )
    out_specs = (
        P(("dp", "tensor"), None),
        P(("dp", "tensor"), None),
        P(),
        P("dp", "tensor"),
        P("dp", "tensor"),
        P("dp", None),
        P("dp", "tensor"),
        P("tensor", "dp"),
        P(None, "tensor"),
        P("tensor"),
        P(),
        P(),
        P("tensor"),
        P("tensor"),
        P("tensor"),
        P("tensor"),
    )
    return jax.shard_map(body, mesh=mesh, in_specs=in_specs, out_specs=out_specs, check_vma=False)
```

```python
from functools import partial

import jax
import jax.numpy as jnp
from jax import lax
from jax.experimental import pallas as pl
from jax.experimental.pallas import tpu as pltpu
from jax.sharding import PartitionSpec as P

BLOCK = 256


EPSILON = 1e-05
SUM_PRECISION = lax.Precision.HIGHEST


def segments(sequence_lengths, sequence_owner, device, row_count):
    owned = (sequence_owner == device).astype(jnp.int32)
    seq_ends = jnp.cumsum(sequence_lengths * owned, dtype=jnp.int32)
    positions = jnp.arange(row_count, dtype=jnp.int32)
    finished = (seq_ends[None, :] <= positions[:, None]) & (owned[None, :] == 1)
    segment = jnp.sum(finished.astype(jnp.int32), axis=1, dtype=jnp.int32)
    present = positions < seq_ends[-1]
    return (segment, present)


def conv_seq(values, kernel, offset_bias, segment):
    kernel_size = kernel.shape[0]
    row_count = values.shape[0]
    result = offset_bias + kernel[kernel_size - 1] * values
    for offset in range(1, kernel_size):
        moved = jnp.pad(values[: row_count - offset], ((offset, 0), (0, 0)))
        before = jnp.pad(segment[: row_count - offset], (offset, 0), constant_values=-1)
        result = (
            result
            + kernel[kernel_size - 1 - offset]
            * moved
            * (before == segment).astype(jnp.float32)[:, None]
        )
    return result


def prepare(
    value_proj,
    bc_proj,
    step_raw,
    conv_value,
    conv_value_bias,
    conv_bc,
    conv_bc_bias,
    step_bias,
    decay_log,
    segment,
):
    values = jax.nn.silu(conv_seq(value_proj, conv_value, conv_value_bias, segment))
    bc_conv = jax.nn.silu(conv_seq(bc_proj, conv_bc, conv_bc_bias, segment))
    state_size = bc_proj.shape[1] // 2
    step_size = jax.nn.softplus(step_raw + step_bias)
    row_count, head_count = step_size.shape
    blocks = row_count // BLOCK
    rates = (step_size * -jnp.exp(decay_log)).reshape(blocks, BLOCK, head_count)
    segment_blocks = segment.reshape(blocks, BLOCK)
    lower_mask = jnp.arange(BLOCK)[:, None] >= jnp.arange(BLOCK)[None, :]
    cum_rates = jnp.einsum(
        "ij,cjh->cih", lower_mask.astype(jnp.float32), rates, precision=SUM_PRECISION
    )
    last_rate = cum_rates[:, -1, :]
    prev_last = jnp.concatenate([jnp.full((1,), -2, jnp.int32), segment_blocks[:-1, -1]])
    tail_mask = (segment_blocks == segment_blocks[:, -1:]).astype(jnp.float32)
    head_same = (segment_blocks == prev_last[:, None]).astype(jnp.float32)
    keep_flag = (segment_blocks[:, -1] == prev_last).astype(jnp.float32)
    tail = jnp.exp(last_rate[:, None, :] - cum_rates) * tail_mask[..., None]
    edge = jnp.exp(cum_rates) * head_same[..., None]
    gain = jnp.exp(last_rate) * keep_flag[:, None]
    flat = (row_count, head_count)
    return (
        values,
        bc_conv[:, :state_size],
        bc_conv[:, state_size:],
        step_size,
        cum_rates.reshape(flat),
        edge.reshape(flat),
        tail.reshape(flat),
        jnp.repeat(gain, values.shape[1] // head_count, axis=1)[:, None, :],
    )


def block_mask(seg_col, seg_row):
    shape = (BLOCK, BLOCK)
    lower = lax.broadcasted_iota(jnp.int32, shape, 0) >= lax.broadcasted_iota(jnp.int32, shape, 1)
    return lower & (seg_col[...] == seg_row[...])


def pick(ref, pair, low_lane):
    return jnp.where(low_lane, ref[:, 2 * pair : 2 * pair + 1], ref[:, 2 * pair + 1 : 2 * pair + 2])


def scan_forward_kernel(
    v, b, c, step, cum, edge, tail, gain, cum_row, seg_col, seg_row, skip, y, prior, state
):
    @pl.when(pl.program_id(0) == 0)
    def _():
        state[...] = jnp.zeros_like(state)

    prior[...] = state[...]
    keys = b[...].astype(jnp.bfloat16)
    queries = c[...].astype(jnp.bfloat16)
    scores = contract_cols(queries, keys)
    mask = block_mask(seg_col, seg_row)
    low_lane = lax.broadcasted_iota(jnp.int32, (BLOCK, 128), 1) < 64
    for pair in range(v.shape[1] // 128):
        cols = slice(128 * pair, 128 * pair + 128)
        values = v[:, cols]
        scaled = values * pick(step, pair, low_lane)
        scaled_low = scaled.astype(jnp.bfloat16)
        inside = []
        for head in (2 * pair, 2 * pair + 1):
            gap = cum[:, head : head + 1] - cum_row[head : head + 1, :]
            weight = scores * jnp.exp(jnp.where(mask, gap, -1e30))
            inside.append(dot_rows(weight.astype(jnp.bfloat16), scaled_low))
        before = state[:, cols]
        carried = dot_rows(queries, before.astype(jnp.bfloat16)) * pick(edge, pair, low_lane)
        y[:, cols] = jnp.where(low_lane, inside[0], inside[1]) + carried + skip[:, cols] * values
        fresh = (scaled * pick(tail, pair, low_lane)).astype(jnp.bfloat16)
        state[:, cols] = gain[0, :, cols] * before + contract_rows(keys, fresh)


def scan_backward_kernel(
    v,
    b,
    c,
    step,
    cum,
    edge,
    tail,
    gain,
    cum_row,
    seg_col,
    seg_row,
    skip,
    dy,
    prior,
    dv,
    db,
    dc,
    dstep,
    dcum,
    dedge,
    dtail,
    dgain,
    dcum_row,
    dskip,
    dstate,
):
    @pl.when(pl.program_id(0) == 0)
    def _():
        dstate[...] = jnp.zeros_like(dstate)

    keys = b[...].astype(jnp.bfloat16)
    queries = c[...].astype(jnp.bfloat16)
    scores = contract_cols(queries, keys)
    mask = block_mask(seg_col, seg_row)
    low_lane = lax.broadcasted_iota(jnp.int32, (BLOCK, 128), 1) < 64
    dscores = jnp.zeros((BLOCK, BLOCK), jnp.float32)
    dqueries = jnp.zeros(c.shape, jnp.float32)
    dkeys = jnp.zeros(b.shape, jnp.float32)

    def put(ref, pair, product):
        low_part = jnp.sum(jnp.where(low_lane, product, 0.0), axis=1, keepdims=True)
        all_part = jnp.sum(product, axis=1, keepdims=True)
        ref[:, 2 * pair : 2 * pair + 1] = low_part
        ref[:, 2 * pair + 1 : 2 * pair + 2] = all_part - low_part

    for pair in range(v.shape[1] // 128):
        cols = slice(128 * pair, 128 * pair + 128)
        values = v[:, cols]
        grad = dy[:, cols]
        step_pair = pick(step, pair, low_lane)
        edge_pair = pick(edge, pair, low_lane)
        tail_pair = pick(tail, pair, low_lane)
        scaled = values * step_pair
        scaled_low = scaled.astype(jnp.bfloat16)
        grad_low = grad.astype(jnp.bfloat16)
        inside = []
        for side in range(2):
            head = 2 * pair + side
            gap = cum[:, head : head + 1] - cum_row[head : head + 1, :]
            decay = jnp.exp(jnp.where(mask, gap, -1e30))
            weight = scores * decay
            own = low_lane if side == 0 else jnp.logical_not(low_lane)
            dweight = contract_cols(jnp.where(own, grad, 0.0).astype(jnp.bfloat16), scaled_low)
            dscores = dscores + dweight * decay
            product = dweight * weight
            dcum[:, head : head + 1] = jnp.sum(product, axis=1, keepdims=True)
            dcum_row[head : head + 1, :] = jnp.sum(product, axis=0, keepdims=True)
            inside.append(contract_rows(weight.astype(jnp.bfloat16), grad_low))
        before = prior[:, cols]
        before_low = before.astype(jnp.bfloat16)
        after = dstate[:, cols]
        after_low = after.astype(jnp.bfloat16)
        put(dedge, pair, grad * dot_rows(queries, before_low))
        key_part = dot_rows(keys, after_low)
        put(dtail, pair, scaled * key_part)
        dscaled = jnp.where(low_lane, inside[0], inside[1]) + tail_pair * key_part
        put(dstep, pair, dscaled * values)
        dv[:, cols] = step_pair * dscaled + skip[:, cols] * grad
        dgain[0, :, cols] = jnp.sum(before * after, axis=0, keepdims=True)
        dskip[0, :, cols] = jnp.sum(grad * values, axis=0, keepdims=True)
        edge_grad = (edge_pair * grad).astype(jnp.bfloat16)
        dqueries = dqueries + contract_cols(edge_grad, before_low)
        dkeys = dkeys + contract_cols((tail_pair * scaled).astype(jnp.bfloat16), after_low)
        dstate[:, cols] = gain[0, :, cols] * after + contract_rows(queries, edge_grad)
    dscores_low = dscores.astype(jnp.bfloat16)
    dc[...] = dqueries + dot_rows(dscores_low, keys)
    db[...] = dkeys + contract_rows(dscores_low, queries)


def scan_specs(rows, width, heads, states, turned):
    blocks = rows // BLOCK

    def at(position):
        return blocks - 1 - position if turned else position

    wide = pl.BlockSpec((BLOCK, width), lambda i: (at(i), 0))
    key = pl.BlockSpec((BLOCK, states), lambda i: (at(i), 0))
    head = pl.BlockSpec((BLOCK, heads), lambda i: (at(i), 0))
    line = pl.BlockSpec((1, 1, width), lambda i: (at(i), 0, 0))
    across = pl.BlockSpec((heads, BLOCK), lambda i: (0, at(i)))
    seg_col = pl.BlockSpec((BLOCK, 1), lambda i: (at(i), 0))
    seg_row = pl.BlockSpec((1, BLOCK), lambda i: (0, at(i)))
    fixed = pl.BlockSpec((1, width), lambda i: (0, 0))
    prior = pl.BlockSpec((states, width), lambda i: (at(i), 0))
    inputs = [wide, key, key, head, head, head, head, line, across, seg_col, seg_row, fixed]
    return inputs, wide, key, head, line, across, prior


def f32(*shape):
    return jax.ShapeDtypeStruct(shape, jnp.float32)


def scan_forward(parts, extra):
    rows, width = parts[0].shape
    states, heads = parts[1].shape[1], parts[3].shape[1]
    blocks = rows // BLOCK
    inputs, wide, key, head, line, across, prior = scan_specs(rows, width, heads, states, False)
    return pl.pallas_call(
        scan_forward_kernel,
        grid=(blocks,),
        in_specs=inputs,
        out_specs=[wide, prior],
        out_shape=[f32(rows, width), f32(blocks * states, width)],
        scratch_shapes=[pltpu.VMEM((states, width), jnp.float32)],
        compiler_params=pltpu.CompilerParams(vmem_limit_bytes=48 * 1024 * 1024),
        name="scan_forward",
    )(*parts, *extra)


def scan_backward(parts, extra, grad_mixed, prior_states):
    rows, width = parts[0].shape
    states, heads = parts[1].shape[1], parts[3].shape[1]
    blocks = rows // BLOCK
    inputs, wide, key, head, line, across, prior = scan_specs(rows, width, heads, states, True)
    return pl.pallas_call(
        scan_backward_kernel,
        grid=(blocks,),
        in_specs=inputs + [wide, prior],
        out_specs=[wide, key, key, head, head, head, head, line, across, line],
        out_shape=[
            f32(rows, width),
            f32(rows, states),
            f32(rows, states),
            f32(rows, heads),
            f32(rows, heads),
            f32(rows, heads),
            f32(rows, heads),
            f32(blocks, 1, width),
            f32(heads, rows),
            f32(blocks, 1, width),
        ],
        scratch_shapes=[pltpu.VMEM((states, width), jnp.float32)],
        compiler_params=pltpu.CompilerParams(vmem_limit_bytes=48 * 1024 * 1024),
        name="scan_backward",
    )(*parts, *extra, grad_mixed, prior_states)


def dot_rows(left_side, right_side):
    return jnp.dot(left_side, right_side, preferred_element_type=jnp.float32)


def contract_rows(left_side, right_side):
    return lax.dot_general(
        left_side, right_side, (((0,), (0,)), ((), ())), preferred_element_type=jnp.float32
    )


def contract_cols(left_side, right_side):
    return lax.dot_general(
        left_side, right_side, (((1,), (1,)), ((), ())), preferred_element_type=jnp.float32
    )


SWAP = ((0, 1), (1, 0))


def swap_gather(own, tensor_index):
    other = lax.ppermute(own, "tensor", SWAP)
    first = jnp.where(tensor_index == 0, own, other)
    second = jnp.where(tensor_index == 0, other, own)
    return jnp.concatenate([first, second], 0)


def swap_scatter(whole, tensor_index):
    half = whole.shape[0] // 2
    own = lax.dynamic_slice_in_dim(whole, tensor_index * half, half, 0)
    away = lax.dynamic_slice_in_dim(whole, (1 - tensor_index) * half, half, 0)
    other = lax.ppermute(away, "tensor", SWAP)
    return (own.astype(jnp.float32) + other.astype(jnp.float32)).astype(jnp.bfloat16)


def widen(local_part, tensor_count, tensor_index):
    axis_last = local_part.ndim - 1
    width_local = local_part.shape[axis_last]
    shape_full = local_part.shape[:axis_last] + (width_local * tensor_count,)
    return lax.dynamic_update_slice_in_dim(
        jnp.zeros(shape_full, jnp.float32), local_part, tensor_index * width_local, axis_last
    )


def narrow(full_part, width_local, tensor_index):
    axis_last = full_part.ndim - 1
    return lax.dynamic_slice_in_dim(full_part, tensor_index * width_local, width_local, axis_last)


def body(
    x_in,
    cotangent,
    sequence_lengths,
    sequence_owner,
    norm_gain,
    proj_gate,
    proj_value,
    proj_bc,
    proj_step,
    proj_out,
    conv_value,
    conv_value_bias,
    conv_bc,
    conv_bc_bias,
    step_bias,
    decay_log,
    skip_gain,
    gate_gain,
):
    half_rows = x_in.shape[0]
    tensor_count = lax.axis_size("tensor")
    row_count = half_rows * tensor_count
    tensor_index = lax.axis_index("tensor")
    device_index = lax.axis_index("dp")
    inner_local = proj_gate.shape[1]
    heads_local = proj_step.shape[1]
    main_cols = 2 * inner_local + heads_local
    inner_all = inner_local * tensor_count
    in_float = x_in.astype(jnp.float32)
    in_rstd = lax.rsqrt(jnp.mean(in_float * in_float, axis=-1, keepdims=True) + EPSILON)
    in_hat = in_float * in_rstd
    normed = (in_hat * norm_gain).astype(jnp.bfloat16)
    side_pack = jnp.concatenate([proj_value, proj_step, proj_bc], 1)
    gate_pack = jnp.concatenate([proj_gate, proj_out.T], 1)
    side_weight = lax.all_gather(side_pack, "dp", axis=0, tiled=True)
    gate_pack = lax.all_gather(gate_pack, "dp", axis=0, tiled=True)
    gate_weight = gate_pack[:, :inner_local]
    out_weight = gate_pack[:, inner_local:]
    normed_all = swap_gather(normed, tensor_index)
    projected = jnp.dot(normed_all, side_weight, preferred_element_type=jnp.float32)
    value_proj = projected[:, :inner_local]
    step_raw = projected[:, inner_local : inner_local + heads_local]
    bc_proj = projected[:, inner_local + heads_local :]
    gate_z = jnp.dot(normed_all, gate_weight, preferred_element_type=jnp.float32)
    segment, present = segments(sequence_lengths, sequence_owner, device_index, row_count)
    present_float = present.astype(jnp.float32)
    parts, prepare_back = jax.vjp(
        partial(prepare, segment=segment),
        value_proj,
        bc_proj,
        step_raw,
        conv_value,
        conv_value_bias,
        conv_bc,
        conv_bc_bias,
        step_bias,
        decay_log,
    )
    extra = (
        parts[4].T,
        segment[:, None],
        segment[None, :],
        jnp.repeat(skip_gain, inner_local // heads_local)[None, :],
    )
    mixed_out, prior_states = scan_forward(parts, extra)
    gate_sigmoid = jax.nn.sigmoid(gate_z)
    silu_gate = gate_z * gate_sigmoid
    gated_out = mixed_out * silu_gate
    squares = lax.psum(jnp.sum(gated_out * gated_out, axis=-1), "tensor")
    gate_scale = lax.rsqrt(squares / inner_all + EPSILON)[:, None]
    gnorm = (gated_out * gate_scale * gate_gain).astype(jnp.bfloat16)
    branch_own = swap_scatter(
        contract_cols(gnorm, out_weight).astype(jnp.bfloat16),
        tensor_index,
    ).astype(jnp.float32)
    present_own = lax.dynamic_slice_in_dim(present_float, tensor_index * half_rows, half_rows, 0)
    block_out = (in_float + present_own[:, None] * branch_own).astype(jnp.bfloat16)
    mask_rows = present_float.astype(jnp.bfloat16)
    masked_cot = swap_gather(cotangent, tensor_index) * mask_rows[:, None]
    part_rows = jnp.dot(masked_cot, out_weight, preferred_element_type=jnp.float32)
    gated_scaled = gated_out * gate_scale
    grad_gate_gain = jnp.sum(part_rows * gated_scaled, axis=0)
    grad_hat = part_rows * gate_gain
    dot_sums = lax.psum(jnp.sum(grad_hat * gated_out, axis=-1), "tensor")
    grad_gated = (
        gate_scale * grad_hat
        - gated_out * (gate_scale * gate_scale * gate_scale) * (dot_sums / inner_all)[:, None]
    )
    grad_mixed = grad_gated * silu_gate
    grad_gate_z = grad_gated * mixed_out * gate_sigmoid * (1.0 + gate_z * (1.0 - gate_sigmoid))
    *part_grads, dcum_row, dskip = scan_backward(parts, extra, grad_mixed, prior_states)
    part_grads[4] = part_grads[4] - dcum_row.T
    (
        grad_value,
        grad_bc_part,
        grad_step,
        g_conv_value,
        g_conv_value_bias,
        g_conv_bc,
        g_conv_bc_bias,
        g_step_bias,
        g_decay_log,
    ) = prepare_back(tuple(part_grads))
    g_skip_gain = jnp.sum(dskip.reshape(-1, heads_local, inner_local // heads_local), axis=(0, 2))
    grad_gate_z = grad_gate_z.astype(jnp.bfloat16)
    early = jnp.concatenate(
        [contract_rows(normed_all, grad_gate_z), contract_rows(masked_cot, gnorm)], 1
    ).astype(jnp.bfloat16)
    early = lax.psum_scatter(early, "dp", scatter_dimension=0, tiled=True).astype(jnp.float32)
    bc_own = swap_scatter(grad_bc_part.astype(jnp.bfloat16), tensor_index)
    grad_main = jnp.concatenate([grad_value, grad_step], 1).astype(jnp.bfloat16)
    late = jnp.concatenate(
        [contract_rows(normed_all, grad_main), contract_rows(normed, bc_own)], 1
    ).astype(jnp.bfloat16)
    late = lax.psum_scatter(late, "dp", scatter_dimension=0, tiled=True).astype(jnp.float32)
    side_cols = inner_local + heads_local
    grad_normed = swap_scatter(
        (
            contract_cols(grad_gate_z, gate_weight)
            + contract_cols(grad_main, side_weight[:, :side_cols])
        ).astype(jnp.bfloat16),
        tensor_index,
    ).astype(jnp.float32) + contract_cols(bc_own, side_weight[:, side_cols:])
    summed = (
        early[:, :inner_local],
        late[:, :inner_local],
        lax.psum(late[:, side_cols:], "tensor"),
        late[:, inner_local:side_cols],
        early[:, inner_local:].T,
    )
    grad_hat_in = grad_normed * norm_gain
    grad_in = in_rstd * (
        grad_hat_in - in_hat * jnp.mean(grad_hat_in * in_hat, axis=-1, keepdims=True)
    )
    grad_in = (grad_in + cotangent.astype(jnp.float32)).astype(jnp.bfloat16)
    gain_part = jnp.sum(grad_normed * in_hat, axis=0)
    small = lax.psum(
        (
            gain_part,
            g_conv_bc,
            g_conv_bc_bias,
            widen(g_conv_value, tensor_count, tensor_index),
            widen(g_conv_value_bias, tensor_count, tensor_index),
            widen(g_step_bias, tensor_count, tensor_index),
            widen(g_decay_log, tensor_count, tensor_index),
            widen(g_skip_gain, tensor_count, tensor_index),
            widen(grad_gate_gain, tensor_count, tensor_index),
        ),
        ("dp", "tensor"),
    )
    return (
        block_out,
        grad_in,
        small[0],
        summed[0],
        summed[1],
        summed[2],
        summed[3],
        summed[4],
        narrow(small[3], inner_local, tensor_index),
        narrow(small[4], inner_local, tensor_index),
        small[1],
        small[2],
        narrow(small[5], heads_local, tensor_index),
        narrow(small[6], heads_local, tensor_index),
        narrow(small[7], heads_local, tensor_index),
        narrow(small[8], inner_local, tensor_index),
    )


def solution(mesh):
    in_specs = (
        P(("dp", "tensor"), None),
        P(("dp", "tensor"), None),
        P(),
        P(),
        P(),
        P("dp", "tensor"),
        P("dp", "tensor"),
        P("dp", None),
        P("dp", "tensor"),
        P("tensor", "dp"),
        P(None, "tensor"),
        P("tensor"),
        P(),
        P(),
        P("tensor"),
        P("tensor"),
        P("tensor"),
        P("tensor"),
    )
    out_specs = (
        P(("dp", "tensor"), None),
        P(("dp", "tensor"), None),
        P(),
        P("dp", "tensor"),
        P("dp", "tensor"),
        P("dp", None),
        P("dp", "tensor"),
        P("tensor", "dp"),
        P(None, "tensor"),
        P("tensor"),
        P(),
        P(),
        P("tensor"),
        P("tensor"),
        P("tensor"),
        P("tensor"),
    )
    return jax.shard_map(body, mesh=mesh, in_specs=in_specs, out_specs=out_specs, check_vma=False)
```
